256 devices in a mesh: blk: 64 (over y, z, x_hi), aux: 4 (over x_lo, core).
Axes of the slice: x: 4 (x_hi: 2, x_lo: 2; x = x_hi * 2 + x_lo), y: 4, z: 8, core: 2. Of those that a mesh axis runs over, the one named last changes fastest.
Arguments:
- basis_three: bfloat16 [256, 512, 12288], P('aux', 'blk'), may hold values from -0.29882812 to 0.29882812
- block_mask: int32 [4, 512, 3], P('aux', 'blk'), may hold values 0 or 1
- density: bfloat16 [32768, 192], P('blk'), as said below
- density_mask: int32 [512, 3], P('blk'), may hold values from 0 to 1, as said below
Outputs:
- exchange: float32 [32768, 192], P(('blk', 'aux'))
The draws below stay inside these ranges and needn't reach their ends.
Inputs may be any that keep to these rules, and one draw needn't show every extreme that they name: density is symmetric as a full periodic banded matrix. `density_mask`: column 1 is 1 everywhere; column 2 of block l equals column 0 of block l + 1 modulo 512, so the masked density stays symmetric.
All inputs are finite; a program needn't handle non-finite values. No bound on the sum of `block_mask` on one device may be relied on, other than what follows from the above.
Results may differ from the reference program's by a relative error of at most 0.013.
Values may be sent and summed in bfloat16 or wider, within the bound.
A program may use at most 128 MiB of HBM per device.

```python
import jax
import jax.numpy as jnp
from jax import lax

BS = 64
AUX = 256
AUXB = 4
NBLK = 512


def draw_density(key, part):
    key = jax.random.fold_in(key, 11)
    first_key, second_key = jax.random.split(key, 2)
    factor = (3.0 * BS) ** (-0.5)
    upper = jax.random.normal(first_key, (NBLK, BS, BS), jnp.float32) * factor
    inner = jax.random.normal(second_key, (NBLK, BS, BS), jnp.float32) * factor
    diagonal = (inner + jnp.transpose(inner, (0, 2, 1))) * 0.7071
    lower = jnp.transpose(jnp.roll(upper, 1, axis=0), (0, 2, 1))
    whole = jnp.concatenate([lower, diagonal, upper], axis=2)
    return whole.reshape(NBLK * BS, 3 * BS).astype(jnp.bfloat16)


def draw_density_mask(key, part):
    key = jax.random.fold_in(key, 7)
    coupling = (jax.random.randint(key, (NBLK,), 0, 4) > 0).astype(jnp.int32)
    middle = jnp.ones((NBLK,), jnp.int32)
    return jnp.stack([jnp.roll(coupling, 1), middle, coupling], axis=1)


def place_ends(array, key, low, largest):
    extent = array.shape
    spot = [jax.random.randint(jax.random.fold_in(key, axis), (), 0, extent[axis]) for axis in range(len(extent))]
    array = array.at[tuple(spot)].set(low)
    longest = extent.index(max(extent))
    spot[longest] = (spot[longest] + 1) % extent[longest]
    return array.at[tuple(spot)].set(largest)


def block_scale(key, dims, pieces, low, top_value):
    factor_of = 1.0
    for axis_at, shards_of in pieces:
        steps = jax.random.uniform(jax.random.fold_in(jax.random.fold_in(key, 6), axis_at), (shards_of,), jnp.float32, low / len(pieces), top_value / len(pieces))
        factor_of = factor_of * jnp.repeat(jnp.exp(steps), dims[axis_at] // shards_of).reshape((-1,) + (1,) * (len(dims) - 1 - axis_at))
    return factor_of


def normal_values(rng, shape, width, limit, cuts=(), held_as=jnp.bfloat16):
    array = width * jax.random.normal(rng, shape, jnp.float32)
    if cuts:
        array = array * block_scale(rng, shape, cuts, -0.22, 0.18)
    return jnp.clip(array, -limit, limit).astype(held_as)


def setup_inputs(seed: int = 0) -> dict:
    seeds = jax.random.split(jax.random.key(seed), 5)
    return {
        "basis_three": normal_values(seeds[0], (AUX, NBLK, 3 * BS * BS), 0.046, 0.29882812, ((0, 4), (1, 64))),
        "block_mask": place_ends((jax.random.randint(seeds[1], (AUXB, NBLK, 3), 0, 4) < 3).astype(jnp.int32), jax.random.fold_in(seeds[1], 1), 0, 1),
        "density": draw_density(jax.random.fold_in(seeds[4], 71), 0),
        "density_mask": draw_density_mask(jax.random.fold_in(seeds[4], 71), 0),
    }


def reference(basis_three, block_mask, density, density_mask):
    block_total = NBLK
    sub_rows = 16
    block_marks = block_mask.astype(jnp.bfloat16)
    three_center = (basis_three.reshape(AUXB, BS, block_total, BS, 3, BS) * block_marks[:, None, :, None, :, None]).reshape(AUX // sub_rows, sub_rows, block_total, BS, 3 * BS)
    density_marks = density_mask.astype(jnp.bfloat16)
    density_masked = (density.reshape(block_total, BS, 3, BS) * density_marks[:, None, :, None]).reshape(block_total, BS, 3 * BS)
    density_wide = density_masked.astype(jnp.float32)

    def add_group(totals, aux_slab):
        slab_wide = aux_slab.astype(jnp.float32)
        partial_x = jnp.zeros((sub_rows, block_total, BS, 5 * BS), jnp.float32)
        for offset in (-1, 0, 1):
            density_near = jnp.roll(density_wide, -offset, axis=0)
            basis_part = slab_wide[..., (offset + 1) * BS:(offset + 2) * BS]
            term = jnp.einsum('qrmk,rks->qrms', basis_part, density_near)
            partial_x = partial_x.at[..., (offset + 1) * BS:(offset + 4) * BS].add(term)
        x_rounded = lax.optimization_barrier(partial_x.astype(jnp.bfloat16)).astype(jnp.float32)
        updated = []
        for position, target in enumerate((-1, 0, 1)):
            near_rows = jnp.roll(slab_wide, -target, axis=1)
            piece = x_rounded[..., (target + 1) * BS:(target + 4) * BS]
            updated.append(totals[position] + jnp.einsum('qrms,qrns->rmn', piece, near_rows))
        return tuple(updated), None

    zeros_k = tuple(jnp.zeros((block_total, BS, BS), jnp.float32) for position in range(3))
    k_blocks, unused = lax.scan(add_group, zeros_k, three_center)
    return jnp.stack(k_blocks, axis=2).reshape(block_total * BS, 3 * BS)
```

```python
import functools

import jax
import jax.numpy as jnp
from jax import lax
from jax.experimental import pallas as pl
from jax.experimental.pallas import tpu as pltpu
from jax.sharding import PartitionSpec as P

MESH = pl.DeviceIdType.MESH
NT = (((1,), (1,)), ((), ()))
BF = jnp.bfloat16
F32 = jnp.float32

NB = 8
BS = 64
CP = 4
NC = 16
NG = NC // 2


def first_place(b):
    return (b + 3) % 4


def aligned(cols, halves, place, low):
    turned = {}

    def at(half, side):
        col = half // 2
        if half % 2 == side:
            return cols[col]
        if col not in turned:
            turned[col] = pltpu.roll(cols[col], BS, 1)
        return turned[col]

    slots = [None] * 4
    for k, half in enumerate(halves):
        slots[(place + k) % 4] = half
    out = []
    for q in range(2):
        left, right = slots[2 * q], slots[2 * q + 1]
        if left is None:
            out.append(at(right, 1))
        elif right is None:
            out.append(at(left, 0))
        else:
            a, b = at(left, 0), at(right, 1)
            out.append(a if a is b else jnp.where(low, a, b))
    return out


def kernel(
    nblk, naux,
    x_hbm, bm_ref, d_hbm, dm_ref, out_ref,
    x_v, d_v, ta, tb, h7, h0, send_l, send_r, recv_r, recv_l, dens, mask, mask_s, halo_s, halo_r,
    k0, k1, kb, xf, xs, r1, c_s, c_r,
    x_sem, d_sem, hs, hr, bs_l, bs_r, br_l, br_r, s1, rs1, s2, rs2,
):
    blk, aux = lax.axis_index("blk"), lax.axis_index("aux")
    right, left = lax.rem(blk + 1, nblk), lax.rem(blk + nblk - 1, nblk)

    def load(c):
        return pltpu.make_async_copy(x_hbm.at[pl.ds(c * CP, CP)], x_v.at[pl.ds(c * CP, CP)], x_sem.at[c])

    density = pltpu.make_async_copy(d_hbm, d_v, d_sem)
    density.start()
    for c in range(NC):
        load(c).start()

    barrier = pltpu.get_barrier_semaphore()
    for where in (left, blk, right):
        for k in range(naux):
            if where is blk and k == 0:
                continue
            pl.semaphore_signal(barrier, inc=1, device_id=(where, lax.rem(aux + k, naux)), device_id_type=MESH)

    lane = lax.broadcasted_iota(jnp.int32, (32, 128), 1)
    low = lane < BS
    low64 = lax.broadcasted_iota(jnp.int32, (BS, 128), 1) < BS

    def lanes_of(values, place, rows):
        spot = lax.broadcasted_iota(jnp.int32, (rows, 256), 1) // BS
        total = jnp.zeros((rows, 256), F32)
        for j, value in enumerate(values):
            total = jnp.where(spot == (place + j) % 4, value, total)
        return total.astype(BF)

    for b in range(NB):
        mask[b] = lanes_of([bm_ref[0, b, j].astype(F32) for j in range(3)], first_place(b), 32)
    for s, b in enumerate((0, NB - 1)):
        m = [bm_ref[0, b, j].astype(F32) for j in range(3)]
        for q, (u, v) in enumerate(((0, 1), (2, 0), (1, 2))):
            mask_s[s, :, q * 128 : (q + 1) * 128] = jnp.where(low, m[u], m[v]).astype(BF)
    hole = [lanes_of([1.0, 1.0, 1.0], first_place(b), 32) for b in (0, NB - 1)]

    density.wait()
    zero = jnp.zeros((BS, 128), BF)

    def rows_of(l):
        cols = [d_v[l * BS : (l + 1) * BS, 0:128], jnp.concatenate([d_v[l * BS : (l + 1) * BS, 128:192], zero[:, 0:BS]], axis=1)]
        m = [dm_ref[l, j].astype(F32) for j in range(3)]
        return [
            cols[0] * jnp.where(low64, m[0], m[1]).astype(BF),
            cols[1] * jnp.where(low64, m[2], 0.0).astype(BF),
        ]

    first, last = rows_of(0), rows_of(NB - 1)
    halo_s[0] = jnp.where(low64, pltpu.roll(first[0], BS, 1), pltpu.roll(first[1], BS, 1))
    halo_s[1] = last[0]

    def to_left(src, dst, ss, rs):
        return pltpu.make_async_remote_copy(src_ref=src, dst_ref=dst, send_sem=ss, recv_sem=rs, device_id=(left, aux), device_id_type=MESH)

    def to_right(src, dst, ss, rs):
        return pltpu.make_async_remote_copy(src_ref=src, dst_ref=dst, send_sem=ss, recv_sem=rs, device_id=(right, aux), device_id_type=MESH)

    halo = (
        to_left(halo_s.at[0], halo_r.at[0], hs.at[0], hr.at[0]),
        to_right(halo_s.at[1], halo_r.at[1], hs.at[1], hr.at[1]),
    )

    def tile_left(g):
        return to_left(send_l.at[g], recv_r.at[g], bs_l.at[g], br_r.at[g])

    def tile_right(g):
        return to_right(send_r.at[g], recv_l.at[g], bs_r.at[g], br_l.at[g])

    def spread(c, t, send, which, g):
        for k in range(CP):
            rows = x_v[c * CP + k].reshape(NB, 32, 384)
            for b in range(NB):
                u = rows[b]
                if b == (0, NB - 1)[which]:
                    send[g, k] = u * mask_s[which]
                cols = [u[:, q * 128 : (q + 1) * 128] for q in range(3)]
                for par in range(2):
                    made = aligned(cols, [3 * par + n for n in range(3)], first_place(b), low)
                    for q in range(2):
                        t[b, k, par * 32 : (par + 1) * 32, q * 128 : (q + 1) * 128] = made[q] * mask[b, :, q * 128 : (q + 1) * 128]

    def pick(o, base):
        s0 = jnp.where(low64, o[base : base + 64, 0:128], o[base + 64 : base + 128, 0:128])
        s1_ = jnp.where(low64, o[base + 128 : base + 192, 128:256], o[base + 192 : base + 256, 128:256])
        return s0 + s1_

    def multiply(t, which, g):
        before = None
        for b in range(NB):
            tile = t[b].reshape(CP * BS, 256)
            half = jnp.dot(tile, dens[b], preferred_element_type=F32).astype(BF)
            if b == 0:
                k0[b] += pick(lax.dot_general(half, tile, NT, preferred_element_type=F32), 0)
                if which == 1:
                    h0[g] = jnp.dot(tile, dens[NB], preferred_element_type=F32).astype(BF)
            else:
                o = lax.dot_general(jnp.concatenate([half, before], axis=0), tile, NT, preferred_element_type=F32)
                k0[b] += pick(o, 0)
                k1[b - 1] += pick(o, 256)
            if b == NB - 1 and which == 0:
                h7[g] = half
            before = half

    load(0).wait()
    spread(0, ta, send_l, 0, 0)
    pl.semaphore_wait(barrier, 3 * naux - 1)
    tile_left(0).start()
    for h in halo:
        h.start()

    k0[...] = jnp.zeros_like(k0)
    k1[...] = jnp.zeros_like(k1)
    kb[...] = jnp.zeros_like(kb)

    def place_rows(b, l, cols, drop):
        at = l % 4
        made = aligned(cols, [0, 1, 2], first_place(l), low64)
        keep = lanes_of([0.0 if drop == j else 1.0 for j in range(3)], first_place(l), BS)
        for q in range(2):
            dens[b, at * BS : (at + 1) * BS, q * 128 : (q + 1) * 128] = made[q] * keep[:, q * 128 : (q + 1) * 128]

    blocks = {l: rows_of(l) for l in range(NB)}
    for b in range(NB):
        at = (b + 2) % 4
        dens[b, at * BS : (at + 1) * BS, :] = jnp.zeros((BS, 256), BF)
        for l in (b - 1, b, b + 1):
            if 0 <= l < NB:
                place_rows(b, l, blocks[l], 0 if l == b - 1 else None)
    dens[NB, 2 * BS : 3 * BS, :] = jnp.zeros((BS, 256), BF)
    place_rows(NB, 0, blocks[0], None)
    place_rows(NB, 1, blocks[1], 2)

    def turned(v):
        full = jnp.concatenate([v.astype(F32), jnp.zeros((BS, 128), F32)], axis=0)
        return full.T[0:BS].astype(BF)

    halo[0].wait_recv()
    halo[1].wait_recv()
    own = turned(last[1])
    middle = pltpu.roll(halo_r[0], BS, 1)
    after = [jnp.where(low64, own, middle), middle]
    place_rows(NB - 1, NB, after, None)
    own = turned(first[0])
    ahead = [halo_r[1], own]
    place_rows(0, -1, ahead, 0)
    place_rows(NB, -1, ahead, None)

    def step(g, carry):
        load(2 * g + 1).wait()
        spread(2 * g + 1, tb, send_r, 1, g)
        multiply(ta, 0, g)
        tile_right(g).start()

        @pl.when(g < NG - 1)
        def _():
            load(2 * g + 2).wait()

        nxt = jnp.minimum(g + 1, NG - 1)
        spread(2 * nxt, ta, send_l if False else send_l, 0, g + 1)
        multiply(tb, 1, g)

        @pl.when(g < NG - 1)
        def _():
            tile_left(g + 1).start()

        return carry

    lax.fori_loop(0, NG, step, 0)

    def folded(a, c):
        return jnp.where(low64, a + pltpu.roll(a, BS, 1), c + pltpu.roll(c, BS, 1))

    r = lax.broadcasted_iota(jnp.int32, (BS, 128), 0)
    c = lax.broadcasted_iota(jnp.int32, (BS, 128), 1)
    row_perm = jnp.where(r == 32 * (c % 2) + c // 2, 1.0, 0.0)[:, 0:BS]
    back = row_perm.T.astype(BF)
    r = lax.broadcasted_iota(jnp.int32, (128, 128), 0)
    c = lax.broadcasted_iota(jnp.int32, (128, 128), 1)
    lane_perm = jnp.where((r % BS == 32 * (c % 2) + (c % BS) // 2) & (r // BS == c // BS), 1.0, 0.0).astype(BF)

    def natural(v):
        v = jnp.dot(v.astype(BF), lane_perm, preferred_element_type=F32).astype(BF)
        return jnp.dot(back, v, preferred_element_type=F32)

    xs[0] = jnp.zeros((BS, 128), BF)
    xf[0] = jnp.zeros((BS, 128), F32)
    for b in range(NB):
        v = natural(folded(k0[b], k1[b]))
        xf[b + 1] = v
        xs[b + 1] = v.astype(BF)
    shares = []
    for k in range(1, naux):
        to = lax.rem(aux + k, naux)
        cp = pltpu.make_async_remote_copy(
            src_ref=xs.at[pl.ds(2 * to, 3)], dst_ref=r1.at[k - 1], send_sem=s1.at[k - 1], recv_sem=rs1.at[k - 1],
            device_id=(blk, to), device_id_type=MESH,
        )
        cp.start()
        shares.append(cp)

    def edge(recv, g, which):
        parts = []
        for k in range(CP):
            u = recv[g, k]
            cols = [u[:, q * 128 : (q + 1) * 128] for q in range(3)]
            for par in range(2):
                made = aligned(cols, [3 * par + n for n in range(3)], first_place((0, NB - 1)[which]), low)
                parts.append(jnp.concatenate([made[q] * hole[which][:, q * 128 : (q + 1) * 128] for q in range(2)], axis=1))
        return jnp.concatenate(parts, axis=0)

    def far(g, carry):
        tile_left(g).wait_recv()
        kb[0] += pick(lax.dot_general(h7[g], edge(recv_r, g, 0), NT, preferred_element_type=F32), 0)
        tile_right(g).wait_recv()
        kb[1] += pick(lax.dot_general(h0[g], edge(recv_l, g, 1), NT, preferred_element_type=F32), 0)
        return carry

    lax.fori_loop(0, NG, far, 0)

    mine = natural(folded(kb[0], kb[1]))
    c_s[...] = mine.astype(BF)

    def corner(n, where, to, slot):
        return pltpu.make_async_remote_copy(
            src_ref=c_s, dst_ref=c_r.at[slot], send_sem=s2.at[n], recv_sem=rs2.at[slot], device_id=(where, to), device_id_type=MESH
        )

    end = naux - 1
    corner(0, right, 0, naux + aux).start()
    corner(1, left, end, naux + aux).start()

    @pl.when(aux != 0)
    def _():
        corner(2, blk, 0, aux).start()

    @pl.when(aux != end)
    def _():
        corner(3, blk, end, aux).start()

    for cp in shares:
        cp.wait_recv()
    total = []
    for j in range(3):
        v = xf[2 * aux + j]
        for k in range(naux - 1):
            v = v + r1[k, j].astype(F32)
        total.append(v)

    def transposed(v):
        return jnp.concatenate([v, jnp.zeros((BS, 128), F32)], axis=0).T

    def store(n, j, v):
        out_ref[n * BS : (n + 1) * BS, j * BS : (j + 1) * BS] = v

    store(0, 0, transposed(total[0])[BS:128, 0:BS])
    store(0, 1, total[1][:, 0:BS])
    store(0, 2, total[1][:, BS:128])
    store(1, 0, transposed(total[1])[BS:128, 0:BS])
    store(1, 1, total[2][:, 0:BS])
    store(1, 2, total[2][:, BS:128])

    def boundary(own_half, slots):
        here, there = mine, jnp.zeros((BS, 128), F32)
        for slot in slots:
            corner(0, blk, 0, slot).wait_recv()
            here = here + c_r[slot].astype(F32)
        for slot in range(naux, 2 * naux):
            corner(0, blk, 0, slot).wait_recv()
            there = there + c_r[slot].astype(F32)
        other = transposed(there)
        if own_half == 1:
            return here[:, BS:128] + other[0:BS, 0:BS]
        return here[:, 0:BS] + other[BS:128, 0:BS]

    @pl.when(aux == 0)
    def _():
        store(0, 0, boundary(1, range(1, naux)))

    @pl.when(aux == end)
    def _():
        store(1, 2, boundary(0, range(end)))

    for h in halo:
        h.wait_send()
    for cp in shares:
        cp.wait_send()
    corner(0, right, 0, naux).wait_send()
    corner(1, left, end, naux).wait_send()

    @pl.when(aux != 0)
    def _():
        corner(2, blk, 0, aux).wait_send()

    @pl.when(aux != end)
    def _():
        corner(3, blk, end, aux).wait_send()

    def drain(g, carry):
        tile_left(g).wait_send()
        tile_right(g).wait_send()
        return carry

    lax.fori_loop(0, NG, drain, 0)


def solution(mesh):
    nblk, naux = mesh.shape["blk"], mesh.shape["aux"]

    def on_device(x, block_mask, density, density_mask):
        sem = pltpu.SemaphoreType.DMA
        return pl.pallas_call(
            functools.partial(kernel, nblk, naux),
            name="exchange",
            out_shape=jax.ShapeDtypeStruct((NB * BS // naux, 3 * BS), F32),
            in_specs=[
                pl.BlockSpec(memory_space=pl.ANY),
                pl.BlockSpec(memory_space=pltpu.SMEM),
                pl.BlockSpec(memory_space=pl.ANY),
                pl.BlockSpec(memory_space=pltpu.SMEM),
            ],
            out_specs=pl.BlockSpec(memory_space=pltpu.VMEM),
            scratch_shapes=[
                pltpu.VMEM(x.shape, BF),
                pltpu.VMEM(density.shape, BF),
                pltpu.VMEM((NB, CP, BS, 256), BF),
                pltpu.VMEM((NB, CP, BS, 256), BF),
                pltpu.VMEM((NG, CP * BS, 256), BF),
                pltpu.VMEM((NG, CP * BS, 256), BF),
                pltpu.VMEM((NG + 1, CP, 32, 384), BF),
                pltpu.VMEM((NG, CP, 32, 384), BF),
                pltpu.VMEM((NG, CP, 32, 384), BF),
                pltpu.VMEM((NG, CP, 32, 384), BF),
                pltpu.VMEM((NB + 1, 256, 256), BF),
                pltpu.VMEM((NB, 32, 256), BF),
                pltpu.VMEM((2, 32, 384), BF),
                pltpu.VMEM((2, BS, 128), BF),
                pltpu.VMEM((2, BS, 128), BF),
                pltpu.VMEM((NB, BS, 128), F32),
                pltpu.VMEM((NB, BS, 128), F32),
                pltpu.VMEM((2, BS, 128), F32),
                pltpu.VMEM((NB + 1, BS, 128), F32),
                pltpu.VMEM((NB + 1, BS, 128), BF),
                pltpu.VMEM((naux - 1, 3, BS, 128), BF),
                pltpu.VMEM((BS, 128), BF),
                pltpu.VMEM((2 * naux, BS, 128), BF),
                sem((NC,)), sem, sem((2,)), sem((2,)), sem((NG,)), sem((NG,)), sem((NG,)), sem((NG,)),
                sem((naux - 1,)), sem((naux - 1,)), sem((4,)), sem((2 * naux,)),
            ],
            compiler_params=pltpu.CompilerParams(
                collective_id=0, has_side_effects=True, vmem_limit_bytes=56 * 2**20
            ),
        )(x, block_mask, density, density_mask)

    placed = (P("aux", "blk", None), P("aux", "blk", None), P("blk", None), P("blk", None))
    return jax.shard_map(
        on_device, mesh=mesh, in_specs=placed, out_specs=P(("blk", "aux"), None), check_vma=False
    )
```

```python
import functools

import jax
import jax.numpy as jnp
from jax import lax
from jax.experimental import pallas as pl
from jax.experimental.pallas import tpu as pltpu
from jax.sharding import PartitionSpec as P

MESH = pl.DeviceIdType.MESH
NT = (((1,), (1,)), ((), ()))
BF = jnp.bfloat16
F32 = jnp.float32

NB = 8
BS = 64
CP = 4
NC = 16
NG = NC // 2
ROW = 16


def first_place(b):
    return (b + 3) % 4


def aligned(cols, halves, place, low):
    turned = {}

    def at(half, side):
        col = half // 2
        if half % 2 == side:
            return cols[col]
        if col not in turned:
            turned[col] = pltpu.roll(cols[col], BS, 1)
        return turned[col]

    slots = [None] * 4
    for k, half in enumerate(halves):
        slots[(place + k) % 4] = half
    out = []
    for q in range(2):
        left, right = slots[2 * q], slots[2 * q + 1]
        if left is None:
            out.append(at(right, 1))
        elif right is None:
            out.append(at(left, 0))
        else:
            a, b = at(left, 0), at(right, 1)
            out.append(a if a is b else jnp.where(low, a, b))
    return out


def kernel(
    nblk, naux,
    x_hbm, bm_hbm, d_hbm, dm_hbm, out_ref,
    x_v, d_v, bm_ref, dm_ref, ta, tb, te, hx, send, recv, dens, mask, mask_s, halo_s, halo_r,
    k0, k1, kb, xf, xs, r1, mine, c_s, c_r,
    x_sem, d_sem, m_sem, hs, hr, bs, br, s1, rs1, s2, rs2,
):
    blk, aux = lax.axis_index("blk"), lax.axis_index("aux")
    right, left = lax.rem(blk + 1, nblk), lax.rem(blk + nblk - 1, nblk)

    def load(c):
        return pltpu.make_async_copy(x_hbm.at[pl.ds(c * CP, CP)], x_v.at[pl.ds(c * CP, CP)], x_sem.at[c])

    load(0).start()
    load(1).start()
    marks = (
        pltpu.make_async_copy(bm_hbm, bm_ref, m_sem.at[0]),
        pltpu.make_async_copy(dm_hbm, dm_ref, m_sem.at[1]),
    )
    for m in marks:
        m.start()

    barrier = pltpu.get_barrier_semaphore()
    for where in (left, blk, right):
        for k in range(naux):
            if where is blk and k == 0:
                continue
            pl.semaphore_signal(barrier, inc=1, device_id=(where, lax.rem(aux + k, naux)), device_id_type=MESH)

    density = pltpu.make_async_copy(d_hbm, d_v, d_sem)
    density.start()
    for c in range(2, NC):
        load(c).start()

    lane = lax.broadcasted_iota(jnp.int32, (32, 128), 1)
    low = lane < BS
    low64 = lax.broadcasted_iota(jnp.int32, (BS, 128), 1) < BS

    for m in marks:
        m.wait()

    def block_marks(b):
        return [bm_ref[j, 0, b].astype(F32) for j in range(3)]

    for s, b in enumerate((0, NB - 1)):
        m = block_marks(b)
        for q, (u, v) in enumerate(((0, 1), (2, 0), (1, 2))):
            mask_s[s, :, q * 128 : (q + 1) * 128] = jnp.where(low, m[u], m[v]).astype(BF)

    def to_left(src, dst, ss, rs):
        return pltpu.make_async_remote_copy(src_ref=src, dst_ref=dst, send_sem=ss, recv_sem=rs, device_id=(left, aux), device_id_type=MESH)

    def to_right(src, dst, ss, rs):
        return pltpu.make_async_remote_copy(src_ref=src, dst_ref=dst, send_sem=ss, recv_sem=rs, device_id=(right, aux), device_id_type=MESH)

    halo = (
        to_left(halo_s.at[0], halo_r.at[0], hs.at[0], hr.at[0]),
        to_right(halo_s.at[1], halo_r.at[1], hs.at[1], hr.at[1]),
    )

    def tile(side, g):
        return pltpu.make_async_remote_copy(
            src_ref=send.at[side, g], dst_ref=recv.at[1 - side, g], send_sem=bs.at[side, g], recv_sem=br.at[1 - side, g],
            device_id=(jnp.where(side == 0, left, right), aux), device_id_type=MESH,
        )

    def extract(g, which):
        for k in range(CP):
            rows = x_v[(2 * g + which) * CP + k].reshape(NB, 32, 384)
            send[which, g, k] = rows[(0, NB - 1)[which]] * mask_s[which]

    def spread(c, t):
        for k in range(CP):
            rows = x_v[c * CP + k].reshape(NB, 32, 384)
            for b in range(NB):
                u = rows[b]
                cols = [u[:, q * 128 : (q + 1) * 128] for q in range(3)]
                for par in range(2):
                    made = aligned(cols, [3 * par + n for n in range(3)], first_place(b), low)
                    for q in range(2):
                        rows_of, lanes = slice(par * 32, (par + 1) * 32), slice(q * 128, (q + 1) * 128)
                        v = made[q] * mask[b, :, lanes]
                        t[b, k, rows_of, lanes] = v
                        if b in (0, NB - 1):
                            te[b // (NB - 1), c, k, rows_of, lanes] = v

    def pick(o, base):
        s0 = jnp.where(low64, o[base : base + 64, 0:128], o[base + 64 : base + 128, 0:128])
        s1_ = jnp.where(low64, o[base + 128 : base + 192, 128:256], o[base + 192 : base + 256, 128:256])
        return s0 + s1_

    def product(left, tile):
        return lax.dot_general(left, tile, NT, preferred_element_type=F32)

    def halved(tile, slot):
        return jnp.dot(tile, dens[slot], preferred_element_type=F32).astype(BF)

    def multiply(t):
        before = None
        for b in range(NB):
            tile = t[b].reshape(CP * BS, 256)
            if b == NB - 1:
                k1[b - 1] += pick(product(before, tile), 0)
                continue
            half = halved(tile, b)
            if b > 0:
                o = product(jnp.concatenate([half, before], axis=0), tile)
                k0[b] += pick(o, 0)
                k1[b - 1] += pick(o, CP * BS)
            before = half

    def ends(g, carry):
        for c in range(2):
            first_tile = te[0, 2 * g + c].reshape(CP * BS, 256)
            last_tile = te[1, 2 * g + c].reshape(CP * BS, 256)
            first_half, last_half = halved(first_tile, NB), halved(last_tile, NB - 1)
            k0[0] += pick(product(first_half, first_tile), 0)
            k0[NB - 1] += pick(product(last_half, last_tile), 0)
            if c == 0:
                hx[1, g] = last_half
            else:
                hx[0, g] = first_half
        return carry

    for c in range(2):
        load(c).wait()
        extract(0, c)
        if c == 0:
            pl.semaphore_wait(barrier, 3 * naux - 1)
        tile(c, 0).start()

    density.wait()
    cols = []
    for j in range(3):
        cols.append([])
        for m in range(NB // 2):
            marks_of = jnp.where(low64, dm_ref[j, 2 * m].astype(F32), dm_ref[j, 2 * m + 1].astype(F32)).astype(BF)
            cols[j].append(d_v[j * BS : (j + 1) * BS, m * 128 : (m + 1) * 128] * marks_of)
    halo_s[0] = jnp.where(low64, cols[1][0], cols[0][0])
    halo_s[1] = jnp.where(low64, cols[2][-1], cols[1][-1])
    halo = (
        to_left(halo_s.at[0], halo_r.at[0], hs.at[0], hr.at[0]),
        to_right(halo_s.at[1], halo_r.at[1], hs.at[1], hr.at[1]),
    )

    for h in halo:
        h.start()

    def move(g, carry):
        for c in range(2):
            load(2 * g + c).wait()
            extract(g, c)
            tile(c, g).start()
        return carry

    lax.fori_loop(1, NG, move, 0)

    def lanes_of(values, place, rows):
        spot = lax.broadcasted_iota(jnp.int32, (rows, 256), 1) // BS
        total = jnp.zeros((rows, 256), F32)
        for j, value in enumerate(values):
            total = jnp.where(spot == (place + j) % 4, value, total)
        return total.astype(BF)

    for b in range(NB):
        mask[b] = lanes_of(block_marks(b), first_place(b), 32)
    hole = [lanes_of([1.0, 1.0, 1.0], first_place(b), 32) for b in (0, NB - 1)]

    k0[...] = jnp.zeros_like(k0)
    k1[...] = jnp.zeros_like(k1)
    kb[...] = jnp.zeros_like(kb)

    def turned(v):
        full = jnp.concatenate([v.astype(F32), jnp.zeros((BS, 128), F32)], axis=0).T
        return jnp.where(low64, full[0:BS], pltpu.roll(full[BS:128], BS, 1)).astype(BF)

    none = jnp.zeros((BS, 128), BF)
    after_t, ahead_t = turned(cols[2][-1]), turned(cols[0][0])
    after_t = pltpu.roll(after_t.astype(F32), BS, 1).astype(BF)
    ahead_t = pltpu.roll(ahead_t.astype(F32), BS, 1).astype(BF)

    def entry(l, c, after, ahead):
        j = l - c + 1
        if not 0 <= j <= 2:
            return none
        if 0 <= c < NB:
            return cols[j][c // 2]
        if c == NB:
            return (after_t, after)[l - NB + 1]
        if c == NB + 1:
            return after
        if c == -1:
            return (ahead, ahead_t)[l + 1]
        return ahead

    def second_factor(slot, b, columns, after, ahead):
        for l in range(b - 1, b + 3):
            for q in range(2):
                pair = [none if l == b + 2 else entry(l, c, after, ahead) for c in sorted(columns, key=lambda c: c % 4)[2 * q : 2 * q + 2]]
                made = none if pair[0] is none and pair[1] is none else jnp.where(low64, pair[0], pair[1])
                dens[slot, (l % 4) * BS : (l % 4 + 1) * BS, q * 128 : (q + 1) * 128] = made

    for b in range(NB - 1):
        second_factor(b, b, range(b - 1, b + 3), None, none)

    spread(0, ta)

    def step(g, carry):
        spread(2 * g + 1, tb)
        multiply(ta)
        spread(jnp.minimum(2 * g + 2, NC - 1), ta)
        multiply(tb)
        return carry

    lax.fori_loop(0, NG, step, 0)

    for h in halo:
        h.wait_recv()
    second_factor(NB - 1, NB - 1, range(NB - 2, NB + 2), halo_r[0], None)
    second_factor(NB, 0, range(-2, 2), None, halo_r[1])
    lax.fori_loop(0, NG, ends, 0)

    def folded(a, c):
        return jnp.where(low64, a + pltpu.roll(a, BS, 1), c + pltpu.roll(c, BS, 1))

    r = lax.broadcasted_iota(jnp.int32, (BS, 128), 0)
    c = lax.broadcasted_iota(jnp.int32, (BS, 128), 1)
    row_perm = jnp.where(r == 32 * (c % 2) + c // 2, 1.0, 0.0)[:, 0:BS]
    back = row_perm.T.astype(BF)
    r = lax.broadcasted_iota(jnp.int32, (128, 128), 0)
    c = lax.broadcasted_iota(jnp.int32, (128, 128), 1)
    lane_perm = jnp.where((r % BS == 32 * (c % 2) + (c % BS) // 2) & (r // BS == c // BS), 1.0, 0.0).astype(BF)

    def natural(v):
        v = jnp.dot(v.astype(BF), lane_perm, preferred_element_type=F32).astype(BF)
        return jnp.dot(back, v, preferred_element_type=F32)

    xs[0] = jnp.zeros((BS, 128), BF)
    xf[0] = jnp.zeros((BS, 128), F32)
    for b in range(NB):
        v = natural(folded(k0[b], k1[b]))
        xf[b + 1] = v
        xs[b + 1] = v.astype(BF)
    shares = []
    for k in range(1, naux):
        to = lax.rem(aux + k, naux)
        cp = pltpu.make_async_remote_copy(
            src_ref=xs.at[pl.ds(2 * to, 3)], dst_ref=r1.at[k - 1], send_sem=s1.at[k - 1], recv_sem=rs1.at[k - 1],
            device_id=(blk, to), device_id_type=MESH,
        )
        cp.start()
        shares.append(cp)

    def edge(side, g):
        parts = []
        for k in range(CP):
            u = recv[side, g, k]
            cols = [u[:, q * 128 : (q + 1) * 128] for q in range(3)]
            for par in range(2):
                made = aligned(cols, [3 * par + n for n in range(3)], first_place((NB - 1, 0)[side]), low)
                parts.append(jnp.concatenate([made[q] * hole[1 - side][:, q * 128 : (q + 1) * 128] for q in range(2)], axis=1))
        return jnp.concatenate(parts, axis=0)

    end = naux - 1

    def corner(n, where, to, slot):
        return pltpu.make_async_remote_copy(
            src_ref=c_s.at[n % 2], dst_ref=c_r.at[slot], send_sem=s2.at[n], recv_sem=rs2.at[slot], device_id=(where, to), device_id_type=MESH
        )

    def finish(sides):
        def far(g, carry):
            for side in sides:
                tile(1 - side, g).wait_recv()
                kb[side] += pick(product(hx[side, g], edge(side, g)), 0)
            return carry

        lax.fori_loop(0, NG, far, 0)
        v = natural(folded(kb[1], kb[0]))
        for side in sides:
            mine[side] = v
            c_s[side] = v.astype(BF)
        for side in sides:
            if side == 0:
                corner(0, left, end, naux + aux).start()
            else:
                corner(1, right, 0, naux + aux).start()

            @pl.when(aux != (0, end)[side])
            def _():
                corner(2 + side, blk, (0, end)[side], aux).start()

    last_of_row = lax.rem(blk, ROW) == ROW - 1

    @pl.when(last_of_row)
    def _():
        finish((1,))
        finish((0,))

    @pl.when(jnp.logical_not(last_of_row))
    def _():
        finish((0, 1))

    for cp in shares:
        cp.wait_recv()
    total = []
    for j in range(3):
        v = xf[2 * aux + j]
        for k in range(naux - 1):
            v = v + r1[k, j].astype(F32)
        total.append(v)

    out_ref[0:BS, :] = jnp.where(low64, pltpu.roll(total[0], BS, 1), total[1])
    out_ref[BS : 2 * BS, :] = jnp.where(low64, total[1], pltpu.roll(total[2], BS, 1))
    out_ref[2 * BS : 3 * BS, :] = jnp.concatenate(total[1:], axis=0).T[BS:128]

    def gathered(total, slots):
        for slot in slots:
            corner(0, blk, 0, slot).wait_recv()
            total = total + c_r[slot].astype(F32)
        return total

    def transposed(v):
        return jnp.concatenate([v, jnp.zeros((BS, 128), F32)], axis=0).T[:, 0:BS]

    nothing = jnp.zeros((BS, 128), F32)

    @pl.when(aux == 0)
    def _():
        own = transposed(gathered(mine[0], range(1, naux)))
        out_ref[0:BS, 0:BS] = own[BS:128] + gathered(nothing, range(naux, 2 * naux))[:, 0:BS]

    @pl.when(aux == end)
    def _():
        near = gathered(nothing, range(naux, 2 * naux))[:, BS:128]
        out_ref[2 * BS : 3 * BS, BS:128] = near + transposed(gathered(mine[1], range(end)))[0:BS]

    for h in halo:
        h.wait_send()
    for cp in shares:
        cp.wait_send()
    corner(0, left, end, naux).wait_send()
    corner(1, right, 0, naux).wait_send()

    @pl.when(aux != 0)
    def _():
        corner(2, blk, 0, aux).wait_send()

    @pl.when(aux != end)
    def _():
        corner(3, blk, end, aux).wait_send()

    def drain(g, carry):
        tile(0, g).wait_send()
        tile(1, g).wait_send()
        return carry

    lax.fori_loop(0, NG, drain, 0)


def solution(mesh):
    nblk, naux = mesh.shape["blk"], mesh.shape["aux"]

    def on_device(x, block_mask, density, density_mask):
        block_mask, density, density_mask = block_mask.transpose(2, 0, 1), density.T, density_mask.T
        sem = pltpu.SemaphoreType.DMA
        return pl.pallas_call(
            functools.partial(kernel, nblk, naux),
            name="exchange",
            out_shape=jax.ShapeDtypeStruct((3 * BS, NB * BS // naux), F32),
            in_specs=[pl.BlockSpec(memory_space=pl.ANY)] * 4,
            out_specs=pl.BlockSpec(memory_space=pltpu.VMEM),
            scratch_shapes=[
                pltpu.VMEM(x.shape, BF),
                pltpu.VMEM(density.shape, BF),
                pltpu.SMEM(block_mask.shape, jnp.int32),
                pltpu.SMEM(density_mask.shape, jnp.int32),
                pltpu.VMEM((NB, CP, BS, 256), BF),
                pltpu.VMEM((NB, CP, BS, 256), BF),
                pltpu.VMEM((2, NC, CP, BS, 256), BF),
                pltpu.VMEM((2, NG, CP * BS, 256), BF),
                pltpu.VMEM((2, NG, CP, 32, 384), BF),
                pltpu.VMEM((2, NG, CP, 32, 384), BF),
                pltpu.VMEM((NB + 1, 256, 256), BF),
                pltpu.VMEM((NB, 32, 256), BF),
                pltpu.VMEM((2, 32, 384), BF),
                pltpu.VMEM((2, BS, 128), BF),
                pltpu.VMEM((2, BS, 128), BF),
                pltpu.VMEM((NB, BS, 128), F32),
                pltpu.VMEM((NB, BS, 128), F32),
                pltpu.VMEM((2, BS, 128), F32),
                pltpu.VMEM((NB + 1, BS, 128), F32),
                pltpu.VMEM((NB + 1, BS, 128), BF),
                pltpu.VMEM((naux - 1, 3, BS, 128), BF),
                pltpu.VMEM((2, BS, 128), F32),
                pltpu.VMEM((2, BS, 128), BF),
                pltpu.VMEM((2 * naux, BS, 128), BF),
                sem((NC,)), sem, sem((2,)), sem((2,)), sem((2,)), sem((2, NG)), sem((2, NG)),
                sem((naux - 1,)), sem((naux - 1,)), sem((4,)), sem((2 * naux,)),
            ],
            compiler_params=pltpu.CompilerParams(
                collective_id=0, has_side_effects=True, vmem_limit_bytes=56 * 2**20
            ),
        )(x, block_mask, density, density_mask).T

    placed = (P("aux", "blk", None), P("aux", "blk", None), P("blk", None), P("blk", None))
    return jax.shard_map(
        on_device, mesh=mesh, in_specs=placed, out_specs=P(("blk", "aux"), None), check_vma=False
    )
```

```python
import functools

import jax
import jax.numpy as jnp
from jax import lax
from jax.experimental import pallas as pl
from jax.experimental.pallas import tpu as pltpu
from jax.sharding import PartitionSpec as P

MESH = pl.DeviceIdType.MESH
NT = (((1,), (1,)), ((), ()))
BF = jnp.bfloat16
F32 = jnp.float32

NB = 8
BS = 64
CP = 4
NC = 16
NG = NC // 2
ROW = 16


def first_place(b):
    return (b + 3) % 4


def aligned(cols, halves, place, low):
    turned = {}

    def at(half, side):
        col = half // 2
        if half % 2 == side:
            return cols[col]
        if col not in turned:
            turned[col] = pltpu.roll(cols[col], BS, 1)
        return turned[col]

    slots = [None] * 4
    for k, half in enumerate(halves):
        slots[(place + k) % 4] = half
    out = []
    for q in range(2):
        left, right = slots[2 * q], slots[2 * q + 1]
        if left is None:
            out.append(at(right, 1))
        elif right is None:
            out.append(at(left, 0))
        else:
            a, b = at(left, 0), at(right, 1)
            out.append(a if a is b else jnp.where(low, a, b))
    return out


def kernel(
    nblk, naux,
    x_hbm, bm_hbm, d_hbm, dm_hbm, out_ref,
    x_v, d_v, bm_ref, dm_ref, ta, tb, te, hx, send, recv, dens, mask, mask_s, halo_s, halo_r,
    k0, k1, kb, xf, xs, r1, mine, c_s, c_r,
    x_sem, d_sem, m_sem, hs, hr, ps, pr, bs, br, s1, rs1, s2, rs2,
):
    blk, aux = lax.axis_index("blk"), lax.axis_index("aux")
    right, left = lax.rem(blk + 1, nblk), lax.rem(blk + nblk - 1, nblk)

    def load(c):
        return pltpu.make_async_copy(x_hbm.at[pl.ds(c * CP, CP)], x_v.at[pl.ds(c * CP, CP)], x_sem.at[c])

    load(0).start()
    load(1).start()
    marks = (
        pltpu.make_async_copy(bm_hbm, bm_ref, m_sem.at[0]),
        pltpu.make_async_copy(dm_hbm, dm_ref, m_sem.at[1]),
    )
    for m in marks:
        m.start()

    barrier = pltpu.get_barrier_semaphore()
    for where in (left, blk, right):
        for k in range(naux):
            if where is blk and k == 0:
                continue
            pl.semaphore_signal(barrier, inc=1, device_id=(where, lax.rem(aux + k, naux)), device_id_type=MESH)

    density = pltpu.make_async_copy(d_hbm, d_v, d_sem)
    density.start()
    for c in range(2, NC):
        load(c).start()

    lane = lax.broadcasted_iota(jnp.int32, (32, 128), 1)
    low = lane < BS
    low64 = lax.broadcasted_iota(jnp.int32, (BS, 128), 1) < BS

    for m in marks:
        m.wait()

    def block_marks(b):
        return [bm_ref[j, 0, b].astype(F32) for j in range(3)]

    for s, b in enumerate((0, NB - 1)):
        m = block_marks(b)
        for q, (u, v) in enumerate(((0, 1), (2, 0), (1, 2))):
            mask_s[s, :, q * 128 : (q + 1) * 128] = jnp.where(low, m[u], m[v]).astype(BF)

    def to_left(src, dst, ss, rs):
        return pltpu.make_async_remote_copy(src_ref=src, dst_ref=dst, send_sem=ss, recv_sem=rs, device_id=(left, aux), device_id_type=MESH)

    def to_right(src, dst, ss, rs):
        return pltpu.make_async_remote_copy(src_ref=src, dst_ref=dst, send_sem=ss, recv_sem=rs, device_id=(right, aux), device_id_type=MESH)

    def tile(side, g):
        return pltpu.make_async_remote_copy(
            src_ref=send.at[side, g], dst_ref=recv.at[1 - side, g], send_sem=bs.at[side, g], recv_sem=br.at[1 - side, g],
            device_id=(jnp.where(side == 0, left, right), aux), device_id_type=MESH,
        )

    def extract(g, which):
        for k in range(CP):
            rows = x_v[(2 * g + which) * CP + k].reshape(NB, 32, 384)
            send[which, g, k] = rows[(0, NB - 1)[which]] * mask_s[which]

    def spread(c, t):
        for k in range(CP):
            rows = x_v[c * CP + k].reshape(NB, 32, 384)
            for b in range(NB):
                u = rows[b]
                cols = [u[:, q * 128 : (q + 1) * 128] for q in range(3)]
                for par in range(2):
                    made = aligned(cols, [3 * par + n for n in range(3)], first_place(b), low)
                    for q in range(2):
                        rows_of, lanes = slice(par * 32, (par + 1) * 32), slice(q * 128, (q + 1) * 128)
                        v = made[q] * mask[b, :, lanes]
                        t[b, k, rows_of, lanes] = v
                        if b in (0, NB - 1):
                            te[b // (NB - 1), c, k, rows_of, lanes] = v

    def pick(o, base):
        s0 = jnp.where(low64, o[base : base + 64, 0:128], o[base + 64 : base + 128, 0:128])
        s1_ = jnp.where(low64, o[base + 128 : base + 192, 128:256], o[base + 192 : base + 256, 128:256])
        return s0 + s1_

    def product(left, tile):
        return lax.dot_general(left, tile, NT, preferred_element_type=F32)

    def halved(tile, slot):
        return jnp.dot(tile, dens[slot], preferred_element_type=F32).astype(BF)

    def multiply(t):
        before = None
        for b in range(NB):
            tile = t[b].reshape(CP * BS, 256)
            if b == NB - 1:
                k1[b - 1] += pick(product(before, tile), 0)
                continue
            half = halved(tile, b)
            if b > 0:
                o = product(jnp.concatenate([half, before], axis=0), tile)
                k0[b] += pick(o, 0)
                k1[b - 1] += pick(o, CP * BS)
            before = half

    def ends(g, carry):
        for c in range(2):
            first_tile = te[0, 2 * g + c].reshape(CP * BS, 256)
            last_tile = te[1, 2 * g + c].reshape(CP * BS, 256)
            first_half, last_half = halved(first_tile, NB), halved(last_tile, NB - 1)
            k0[0] += pick(product(first_half, first_tile), 0)
            k0[NB - 1] += pick(product(last_half, last_tile), 0)
            if c == 0:
                hx[1, g] = last_half
            else:
                hx[0, g] = first_half
        return carry

    for c in range(2):
        load(c).wait()
        extract(0, c)
        if c == 0:
            pl.semaphore_wait(barrier, 3 * naux - 1)
        tile(c, 0).start()

    density.wait()
    cols = []
    for j in range(3):
        cols.append([])
        for m in range(NB // 2):
            marks_of = jnp.where(low64, dm_ref[j, 2 * m].astype(F32), dm_ref[j, 2 * m + 1].astype(F32)).astype(BF)
            cols[j].append(d_v[j * BS : (j + 1) * BS, m * 128 : (m + 1) * 128] * marks_of)
    halo_s[0] = jnp.where(low64, cols[1][0], cols[0][0])
    halo_s[1] = jnp.where(low64, cols[2][-1], cols[1][-1])
    core = lax.rem(aux, 2)
    share = pl.ds(pl.multiple_of(core * 32, 32), 32)
    halo = (
        to_left(halo_s.at[0, share], halo_r.at[0, share], hs.at[0], hr.at[0]),
        to_right(halo_s.at[1, share], halo_r.at[1, share], hs.at[1], hr.at[1]),
    )
    passed = [
        pltpu.make_async_remote_copy(
            src_ref=halo_r.at[n, share], dst_ref=halo_r.at[n, share], send_sem=ps.at[n], recv_sem=pr.at[n],
            device_id=(blk, aux + 1 - 2 * core), device_id_type=MESH,
        )
        for n in range(2)
    ]

    for h in halo:
        h.start()

    def move(g, carry):
        for c in range(2):
            load(2 * g + c).wait()
            extract(g, c)
            tile(c, g).start()
        return carry

    lax.fori_loop(1, NG, move, 0)

    def lanes_of(values, place, rows):
        spot = lax.broadcasted_iota(jnp.int32, (rows, 256), 1) // BS
        total = jnp.zeros((rows, 256), F32)
        for j, value in enumerate(values):
            total = jnp.where(spot == (place + j) % 4, value, total)
        return total.astype(BF)

    for b in range(NB):
        mask[b] = lanes_of(block_marks(b), first_place(b), 32)
    hole = [lanes_of([1.0, 1.0, 1.0], first_place(b), 32) for b in (0, NB - 1)]

    k0[...] = jnp.zeros_like(k0)
    k1[...] = jnp.zeros_like(k1)
    kb[...] = jnp.zeros_like(kb)

    def turned(v):
        full = jnp.concatenate([v.astype(F32), jnp.zeros((BS, 128), F32)], axis=0).T
        return jnp.where(low64, full[0:BS], pltpu.roll(full[BS:128], BS, 1)).astype(BF)

    none = jnp.zeros((BS, 128), BF)
    after_t, ahead_t = turned(cols[2][-1]), turned(cols[0][0])
    after_t = pltpu.roll(after_t.astype(F32), BS, 1).astype(BF)
    ahead_t = pltpu.roll(ahead_t.astype(F32), BS, 1).astype(BF)

    def entry(l, c, after, ahead):
        j = l - c + 1
        if not 0 <= j <= 2:
            return none
        if 0 <= c < NB:
            return cols[j][c // 2]
        if c == NB:
            return (after_t, after)[l - NB + 1]
        if c == NB + 1:
            return after
        if c == -1:
            return (ahead, ahead_t)[l + 1]
        return ahead

    def second_factor(slot, b, columns, after, ahead):
        for l in range(b - 1, b + 3):
            for q in range(2):
                pair = [none if l == b + 2 else entry(l, c, after, ahead) for c in sorted(columns, key=lambda c: c % 4)[2 * q : 2 * q + 2]]
                made = none if pair[0] is none and pair[1] is none else jnp.where(low64, pair[0], pair[1])
                dens[slot, (l % 4) * BS : (l % 4 + 1) * BS, q * 128 : (q + 1) * 128] = made

    for b in range(NB - 1):
        second_factor(b, b, range(b - 1, b + 3), None, none)

    spread(0, ta)

    def step(g, carry):
        spread(2 * g + 1, tb)
        multiply(ta)
        spread(jnp.minimum(2 * g + 2, NC - 1), ta)
        multiply(tb)
        return carry

    lax.fori_loop(0, NG, step, 0)

    for h, p in zip(halo, passed, strict=True):
        h.wait_recv()
        p.start()
    for p in passed:
        p.wait()
    second_factor(NB - 1, NB - 1, range(NB - 2, NB + 2), halo_r[0], None)
    second_factor(NB, 0, range(-2, 2), None, halo_r[1])
    lax.fori_loop(0, NG, ends, 0)

    def folded(a, c):
        return jnp.where(low64, a + pltpu.roll(a, BS, 1), c + pltpu.roll(c, BS, 1))

    r = lax.broadcasted_iota(jnp.int32, (BS, 128), 0)
    c = lax.broadcasted_iota(jnp.int32, (BS, 128), 1)
    row_perm = jnp.where(r == 32 * (c % 2) + c // 2, 1.0, 0.0)[:, 0:BS]
    back = row_perm.T.astype(BF)
    r = lax.broadcasted_iota(jnp.int32, (128, 128), 0)
    c = lax.broadcasted_iota(jnp.int32, (128, 128), 1)
    lane_perm = jnp.where((r % BS == 32 * (c % 2) + (c % BS) // 2) & (r // BS == c // BS), 1.0, 0.0).astype(BF)

    def natural(v):
        v = jnp.dot(v.astype(BF), lane_perm, preferred_element_type=F32).astype(BF)
        return jnp.dot(back, v, preferred_element_type=F32)

    xs[0] = jnp.zeros((BS, 128), BF)
    xf[0] = jnp.zeros((BS, 128), F32)
    for b in range(NB):
        v = natural(folded(k0[b], k1[b]))
        xf[b + 1] = v
        xs[b + 1] = v.astype(BF)
    shares = []
    for k in range(1, naux):
        to = lax.rem(aux + k, naux)
        cp = pltpu.make_async_remote_copy(
            src_ref=xs.at[pl.ds(2 * to, 3)], dst_ref=r1.at[k - 1], send_sem=s1.at[k - 1], recv_sem=rs1.at[k - 1],
            device_id=(blk, to), device_id_type=MESH,
        )
        cp.start()
        shares.append(cp)

    def edge(side, g):
        parts = []
        for k in range(CP):
            u = recv[side, g, k]
            cols = [u[:, q * 128 : (q + 1) * 128] for q in range(3)]
            for par in range(2):
                made = aligned(cols, [3 * par + n for n in range(3)], first_place((NB - 1, 0)[side]), low)
                parts.append(jnp.concatenate([made[q] * hole[1 - side][:, q * 128 : (q + 1) * 128] for q in range(2)], axis=1))
        return jnp.concatenate(parts, axis=0)

    end = naux - 1

    def corner(n, where, to, slot):
        return pltpu.make_async_remote_copy(
            src_ref=c_s.at[n % 2], dst_ref=c_r.at[slot], send_sem=s2.at[n], recv_sem=rs2.at[slot], device_id=(where, to), device_id_type=MESH
        )

    def finish(sides):
        def far(g, carry):
            for side in sides:
                tile(1 - side, g).wait_recv()
                kb[side] += pick(product(hx[side, g], edge(side, g)), 0)
            return carry

        lax.fori_loop(0, NG, far, 0)
        v = natural(folded(kb[1], kb[0]))
        for side in sides:
            mine[side] = v
            c_s[side] = v.astype(BF)
        for side in sides:
            if side == 0:
                corner(0, left, end, naux + aux).start()
            else:
                corner(1, right, 0, naux + aux).start()

            @pl.when(aux != (0, end)[side])
            def _():
                corner(2 + side, blk, (0, end)[side], aux).start()

    last_of_row = lax.rem(blk, ROW) == ROW - 1

    @pl.when(last_of_row)
    def _():
        finish((1,))
        finish((0,))

    middle_of_row = lax.rem(blk, ROW) == ROW // 2

    @pl.when(middle_of_row)
    def _():
        finish((0,))
        finish((1,))

    @pl.when(jnp.logical_not(jnp.logical_or(last_of_row, middle_of_row)))
    def _():
        finish((0, 1))

    for cp in shares:
        cp.wait_recv()
    total = []
    for j in range(3):
        v = xf[2 * aux + j]
        for k in range(naux - 1):
            v = v + r1[k, j].astype(F32)
        total.append(v)

    out_ref[0:BS, :] = jnp.where(low64, pltpu.roll(total[0], BS, 1), total[1])
    out_ref[BS : 2 * BS, :] = jnp.where(low64, total[1], pltpu.roll(total[2], BS, 1))
    out_ref[2 * BS : 3 * BS, :] = jnp.concatenate(total[1:], axis=0).T[BS:128]

    def gathered(total, slots):
        for slot in slots:
            corner(0, blk, 0, slot).wait_recv()
            total = total + c_r[slot].astype(F32)
        return total

    def transposed(v):
        return jnp.concatenate([v, jnp.zeros((BS, 128), F32)], axis=0).T[:, 0:BS]

    nothing = jnp.zeros((BS, 128), F32)

    @pl.when(aux == 0)
    def _():
        own = transposed(gathered(mine[0], range(1, naux)))
        out_ref[0:BS, 0:BS] = own[BS:128] + gathered(nothing, range(naux, 2 * naux))[:, 0:BS]

    @pl.when(aux == end)
    def _():
        near = gathered(nothing, range(naux, 2 * naux))[:, BS:128]
        out_ref[2 * BS : 3 * BS, BS:128] = near + transposed(gathered(mine[1], range(end)))[0:BS]

    for h in halo:
        h.wait_send()
    for cp in shares:
        cp.wait_send()
    corner(0, left, end, naux).wait_send()
    corner(1, right, 0, naux).wait_send()

    @pl.when(aux != 0)
    def _():
        corner(2, blk, 0, aux).wait_send()

    @pl.when(aux != end)
    def _():
        corner(3, blk, end, aux).wait_send()

    def drain(g, carry):
        tile(0, g).wait_send()
        tile(1, g).wait_send()
        return carry

    lax.fori_loop(0, NG, drain, 0)


def solution(mesh):
    nblk, naux = mesh.shape["blk"], mesh.shape["aux"]

    def on_device(x, block_mask, density, density_mask):
        block_mask, density, density_mask = block_mask.transpose(2, 0, 1), density.T, density_mask.T
        sem = pltpu.SemaphoreType.DMA
        return pl.pallas_call(
            functools.partial(kernel, nblk, naux),
            name="exchange",
            out_shape=pltpu.VMEM((3 * BS, NB * BS // naux), F32),
            in_specs=[pl.BlockSpec(memory_space=pl.ANY)] * 4,
            out_specs=pl.BlockSpec(memory_space=pltpu.VMEM),
            scratch_shapes=[
                pltpu.VMEM(x.shape, BF),
                pltpu.VMEM(density.shape, BF),
                pltpu.SMEM(block_mask.shape, jnp.int32),
                pltpu.SMEM(density_mask.shape, jnp.int32),
                pltpu.VMEM((NB, CP, BS, 256), BF),
                pltpu.VMEM((NB, CP, BS, 256), BF),
                pltpu.VMEM((2, NC, CP, BS, 256), BF),
                pltpu.VMEM((2, NG, CP * BS, 256), BF),
                pltpu.VMEM((2, NG, CP, 32, 384), BF),
                pltpu.VMEM((2, NG, CP, 32, 384), BF),
                pltpu.VMEM((NB + 1, 256, 256), BF),
                pltpu.VMEM((NB, 32, 256), BF),
                pltpu.VMEM((2, 32, 384), BF),
                pltpu.VMEM((2, BS, 128), BF),
                pltpu.VMEM((2, BS, 128), BF),
                pltpu.VMEM((NB, BS, 128), F32),
                pltpu.VMEM((NB, BS, 128), F32),
                pltpu.VMEM((2, BS, 128), F32),
                pltpu.VMEM((NB + 1, BS, 128), F32),
                pltpu.VMEM((NB + 1, BS, 128), BF),
                pltpu.VMEM((naux - 1, 3, BS, 128), BF),
                pltpu.VMEM((2, BS, 128), F32),
                pltpu.VMEM((2, BS, 128), BF),
                pltpu.VMEM((2 * naux, BS, 128), BF),
                sem((NC,)), sem, sem((2,)), sem((2,)), sem((2,)), sem((2,)), sem((2,)), sem((2, NG)), sem((2, NG)),
                sem((naux - 1,)), sem((naux - 1,)), sem((4,)), sem((2 * naux,)),
            ],
            compiler_params=pltpu.CompilerParams(
                collective_id=0, has_side_effects=True, vmem_limit_bytes=56 * 2**20
            ),
        )(x, block_mask, density, density_mask).T

    placed = (P("aux", "blk", None), P("aux", "blk", None), P("blk", None), P("blk", None))
    return jax.shard_map(
        on_device, mesh=mesh, in_specs=placed, out_specs=P(("blk", "aux"), None), check_vma=False
    )
```

```python
import functools

import jax
import jax.numpy as jnp
from jax import lax
from jax.experimental import pallas as pl
from jax.experimental.pallas import tpu as pltpu
from jax.sharding import PartitionSpec as P

MESH = pl.DeviceIdType.MESH
NT = (((1,), (1,)), ((), ()))
BF = jnp.bfloat16
F32 = jnp.float32

NB = 8
BS = 64
CP = 4
NC = 16
NG = NC // 2


def first_place(b):
    return (b + 3) % 4


def aligned(cols, halves, place, low):
    turned = {}

    def at(half, side):
        col = half // 2
        if half % 2 == side:
            return cols[col]
        if col not in turned:
            turned[col] = pltpu.roll(cols[col], BS, 1)
        return turned[col]

    slots = [None] * 4
    for k, half in enumerate(halves):
        slots[(place + k) % 4] = half
    out = []
    for q in range(2):
        left, right = slots[2 * q], slots[2 * q + 1]
        if left is None:
            out.append(at(right, 1))
        elif right is None:
            out.append(at(left, 0))
        else:
            a, b = at(left, 0), at(right, 1)
            out.append(a if a is b else jnp.where(low, a, b))
    return out


def kernel(
    nblk, naux,
    x_hbm, bm_hbm, d_hbm, dm_hbm, out_ref,
    x_v, d_v, bm_ref, dm_ref, ta, tb, te, hx, send, recv, dens, mask, mask_s, halo_s, halo_r,
    k0, k1, kb, xf, xs, r1, mine, c_s, c_r,
    x_sem, d_sem, m_sem, hs, hr, ps, pr, bs, br, s1, rs1, s2, rs2,
):
    blk, aux = lax.axis_index("blk"), lax.axis_index("aux")
    right, left = lax.rem(blk + 1, nblk), lax.rem(blk + nblk - 1, nblk)

    def load(c):
        return pltpu.make_async_copy(x_hbm.at[pl.ds(c * CP, CP)], x_v.at[pl.ds(c * CP, CP)], x_sem.at[c])

    load(0).start()
    load(1).start()
    marks = (
        pltpu.make_async_copy(bm_hbm, bm_ref, m_sem.at[0]),
        pltpu.make_async_copy(dm_hbm, dm_ref, m_sem.at[1]),
    )
    for m in marks:
        m.start()

    barrier = pltpu.get_barrier_semaphore()
    for where in (left, blk, right):
        for k in range(naux):
            if where is blk and k == 0:
                continue
            pl.semaphore_signal(barrier, inc=1, device_id=(where, lax.rem(aux + k, naux)), device_id_type=MESH)

    density = pltpu.make_async_copy(d_hbm, d_v, d_sem)
    density.start()
    for c in range(2, NC):
        load(c).start()

    lane = lax.broadcasted_iota(jnp.int32, (32, 128), 1)
    low = lane < BS
    low64 = lax.broadcasted_iota(jnp.int32, (BS, 128), 1) < BS

    for m in marks:
        m.wait()

    def block_marks(b):
        return [bm_ref[j, 0, b].astype(F32) for j in range(3)]

    for s, b in enumerate((0, NB - 1)):
        m = block_marks(b)
        for q, (u, v) in enumerate(((0, 1), (2, 0), (1, 2))):
            mask_s[s, :, q * 128 : (q + 1) * 128] = jnp.where(low, m[u], m[v]).astype(BF)

    def to_left(src, dst, ss, rs):
        return pltpu.make_async_remote_copy(src_ref=src, dst_ref=dst, send_sem=ss, recv_sem=rs, device_id=(left, aux), device_id_type=MESH)

    def to_right(src, dst, ss, rs):
        return pltpu.make_async_remote_copy(src_ref=src, dst_ref=dst, send_sem=ss, recv_sem=rs, device_id=(right, aux), device_id_type=MESH)

    def tile(side, g):
        return pltpu.make_async_remote_copy(
            src_ref=send.at[side, g], dst_ref=recv.at[1 - side, g], send_sem=bs.at[side, g], recv_sem=br.at[1 - side, g],
            device_id=(jnp.where(side == 0, left, right), aux), device_id_type=MESH,
        )

    def extract(g, which):
        for k in range(CP):
            rows = x_v[(2 * g + which) * CP + k].reshape(NB, 32, 384)
            send[which, g, k] = rows[(0, NB - 1)[which]] * mask_s[which]

    def spread(c, t):
        for k in range(CP):
            rows = x_v[c * CP + k].reshape(NB, 32, 384)
            for b in range(NB):
                u = rows[b]
                cols = [u[:, q * 128 : (q + 1) * 128] for q in range(3)]
                for par in range(2):
                    made = aligned(cols, [3 * par + n for n in range(3)], first_place(b), low)
                    for q in range(2):
                        rows_of, lanes = slice(par * 32, (par + 1) * 32), slice(q * 128, (q + 1) * 128)
                        v = made[q] * mask[b, :, lanes]
                        t[b, k, rows_of, lanes] = v
                        if b in (0, NB - 1):
                            te[b // (NB - 1), c, k, rows_of, lanes] = v

    def pick(o, base):
        s0 = jnp.where(low64, o[base : base + 64, 0:128], o[base + 64 : base + 128, 0:128])
        s1_ = jnp.where(low64, o[base + 128 : base + 192, 128:256], o[base + 192 : base + 256, 128:256])
        return s0 + s1_

    def product(left, tile):
        return lax.dot_general(left, tile, NT, preferred_element_type=F32)

    def halved(tile, slot):
        return jnp.dot(tile, dens[slot], preferred_element_type=F32).astype(BF)

    def multiply(t):
        before = None
        for b in range(NB):
            tile = t[b].reshape(CP * BS, 256)
            if b == NB - 1:
                k1[b - 1] += pick(product(before, tile), 0)
                continue
            half = halved(tile, b)
            if b > 0:
                o = product(jnp.concatenate([half, before], axis=0), tile)
                k0[b] += pick(o, 0)
                k1[b - 1] += pick(o, CP * BS)
            before = half

    def ends(g, carry):
        for c in range(2):
            first_tile = te[0, 2 * g + c].reshape(CP * BS, 256)
            last_tile = te[1, 2 * g + c].reshape(CP * BS, 256)
            first_half, last_half = halved(first_tile, NB), halved(last_tile, NB - 1)
            k0[0] += pick(product(first_half, first_tile), 0)
            k0[NB - 1] += pick(product(last_half, last_tile), 0)
            if c == 0:
                hx[1, g] = last_half
            else:
                hx[0, g] = first_half
        return carry

    for c in range(2):
        load(c).wait()
        extract(0, c)
        if c == 0:
            pl.semaphore_wait(barrier, 3 * naux - 1)
        tile(c, 0).start()

    density.wait()
    cols = []
    for j in range(3):
        cols.append([])
        for m in range(NB // 2):
            marks_of = jnp.where(low64, dm_ref[j, 2 * m].astype(F32), dm_ref[j, 2 * m + 1].astype(F32)).astype(BF)
            cols[j].append(d_v[j * BS : (j + 1) * BS, m * 128 : (m + 1) * 128] * marks_of)
    halo_s[0] = jnp.where(low64, cols[1][0], cols[0][0])
    halo_s[1] = jnp.where(low64, cols[2][-1], cols[1][-1])
    core = lax.rem(aux, 2)
    share = pl.ds(pl.multiple_of(core * 32, 32), 32)
    halo = (
        to_left(halo_s.at[0, share], halo_r.at[0, share], hs.at[0], hr.at[0]),
        to_right(halo_s.at[1, share], halo_r.at[1, share], hs.at[1], hr.at[1]),
    )
    passed = [
        pltpu.make_async_remote_copy(
            src_ref=halo_r.at[n, share], dst_ref=halo_r.at[n, share], send_sem=ps.at[n], recv_sem=pr.at[n],
            device_id=(blk, aux + 1 - 2 * core), device_id_type=MESH,
        )
        for n in range(2)
    ]

    for h in halo:
        h.start()

    def move(g, carry):
        for c in range(2):
            load(2 * g + c).wait()
            extract(g, c)
            tile(c, g).start()
        return carry

    lax.fori_loop(1, NG, move, 0)

    def lanes_of(values, place, rows):
        spot = lax.broadcasted_iota(jnp.int32, (rows, 256), 1) // BS
        total = jnp.zeros((rows, 256), F32)
        for j, value in enumerate(values):
            total = jnp.where(spot == (place + j) % 4, value, total)
        return total.astype(BF)

    for b in range(NB):
        mask[b] = lanes_of(block_marks(b), first_place(b), 32)
    hole = [lanes_of([1.0, 1.0, 1.0], first_place(b), 32) for b in (0, NB - 1)]

    k0[...] = jnp.zeros_like(k0)
    k1[...] = jnp.zeros_like(k1)
    kb[...] = jnp.zeros_like(kb)

    def turned(v):
        full = jnp.concatenate([v.astype(F32), jnp.zeros((BS, 128), F32)], axis=0).T
        return jnp.where(low64, full[0:BS], pltpu.roll(full[BS:128], BS, 1)).astype(BF)

    none = jnp.zeros((BS, 128), BF)
    after_t, ahead_t = turned(cols[2][-1]), turned(cols[0][0])
    after_t = pltpu.roll(after_t.astype(F32), BS, 1).astype(BF)
    ahead_t = pltpu.roll(ahead_t.astype(F32), BS, 1).astype(BF)

    def entry(l, c, after, ahead):
        j = l - c + 1
        if not 0 <= j <= 2:
            return none
        if 0 <= c < NB:
            return cols[j][c // 2]
        if c == NB:
            return (after_t, after)[l - NB + 1]
        if c == NB + 1:
            return after
        if c == -1:
            return (ahead, ahead_t)[l + 1]
        return ahead

    def second_factor(slot, b, columns, after, ahead):
        for l in range(b - 1, b + 3):
            for q in range(2):
                pair = [none if l == b + 2 else entry(l, c, after, ahead) for c in sorted(columns, key=lambda c: c % 4)[2 * q : 2 * q + 2]]
                made = none if pair[0] is none and pair[1] is none else jnp.where(low64, pair[0], pair[1])
                dens[slot, (l % 4) * BS : (l % 4 + 1) * BS, q * 128 : (q + 1) * 128] = made

    for b in range(NB - 1):
        second_factor(b, b, range(b - 1, b + 3), None, none)

    spread(0, ta)

    def step(g, carry):
        spread(2 * g + 1, tb)
        multiply(ta)
        spread(jnp.minimum(2 * g + 2, NC - 1), ta)
        multiply(tb)
        return carry

    lax.fori_loop(0, NG, step, 0)

    for h, p in zip(halo, passed, strict=True):
        h.wait_recv()
        p.start()
    for p in passed:
        p.wait()
    second_factor(NB - 1, NB - 1, range(NB - 2, NB + 2), halo_r[0], None)
    second_factor(NB, 0, range(-2, 2), None, halo_r[1])
    lax.fori_loop(0, NG, ends, 0)

    def folded(a, c):
        return jnp.where(low64, a + pltpu.roll(a, BS, 1), c + pltpu.roll(c, BS, 1))

    r = lax.broadcasted_iota(jnp.int32, (BS, 128), 0)
    c = lax.broadcasted_iota(jnp.int32, (BS, 128), 1)
    row_perm = jnp.where(r == 32 * (c % 2) + c // 2, 1.0, 0.0)[:, 0:BS]
    back = row_perm.T.astype(BF)
    r = lax.broadcasted_iota(jnp.int32, (128, 128), 0)
    c = lax.broadcasted_iota(jnp.int32, (128, 128), 1)
    lane_perm = jnp.where((r % BS == 32 * (c % 2) + (c % BS) // 2) & (r // BS == c // BS), 1.0, 0.0).astype(BF)

    def natural(v):
        v = jnp.dot(v.astype(BF), lane_perm, preferred_element_type=F32).astype(BF)
        return jnp.dot(back, v, preferred_element_type=F32)

    xs[0] = jnp.zeros((BS, 128), BF)
    xf[0] = jnp.zeros((BS, 128), F32)
    for b in range(NB):
        v = natural(folded(k0[b], k1[b]))
        xf[b + 1] = v
        xs[b + 1] = v.astype(BF)
    shares = []
    for k in range(1, naux):
        to = lax.rem(aux + k, naux)
        cp = pltpu.make_async_remote_copy(
            src_ref=xs.at[pl.ds(2 * to, 3)], dst_ref=r1.at[k - 1], send_sem=s1.at[k - 1], recv_sem=rs1.at[k - 1],
            device_id=(blk, to), device_id_type=MESH,
        )
        cp.start()
        shares.append(cp)

    def edge(side, g):
        parts = []
        for k in range(CP):
            u = recv[side, g, k]
            cols = [u[:, q * 128 : (q + 1) * 128] for q in range(3)]
            for par in range(2):
                made = aligned(cols, [3 * par + n for n in range(3)], first_place((NB - 1, 0)[side]), low)
                parts.append(jnp.concatenate([made[q] * hole[1 - side][:, q * 128 : (q + 1) * 128] for q in range(2)], axis=1))
        return jnp.concatenate(parts, axis=0)

    end = naux - 1

    def corner(n, where, to, slot):
        return pltpu.make_async_remote_copy(
            src_ref=c_s.at[n % 2], dst_ref=c_r.at[slot], send_sem=s2.at[n], recv_sem=rs2.at[slot], device_id=(where, to), device_id_type=MESH
        )

    def finish(sides):
        def far(g, carry):
            for side in sides:
                tile(1 - side, g).wait_recv()
                kb[side] += pick(product(hx[side, g], edge(side, g)), 0)
            return carry

        lax.fori_loop(0, NG, far, 0)
        v = natural(folded(kb[1], kb[0]))
        for side in sides:
            mine[side] = v
            c_s[side] = v.astype(BF)
        for side in sides:
            if side == 0:
                corner(0, left, end, naux + aux).start()
            else:
                corner(1, right, 0, naux + aux).start()

            @pl.when(aux != (0, end)[side])
            def _():
                corner(2 + side, blk, (0, end)[side], aux).start()

    odd = lax.rem(blk, 2) == 1

    @pl.when(odd)
    def _():
        finish((1,))
        finish((0,))

    @pl.when(jnp.logical_not(odd))
    def _():
        finish((0,))
        finish((1,))

    for cp in shares:
        cp.wait_recv()
    total = []
    for j in range(3):
        v = xf[2 * aux + j]
        for k in range(naux - 1):
            v = v + r1[k, j].astype(F32)
        total.append(v)

    out_ref[0:BS, :] = jnp.where(low64, pltpu.roll(total[0], BS, 1), total[1])
    out_ref[BS : 2 * BS, :] = jnp.where(low64, total[1], pltpu.roll(total[2], BS, 1))
    out_ref[2 * BS : 3 * BS, :] = jnp.concatenate(total[1:], axis=0).T[BS:128]

    def gathered(total, slots):
        for slot in slots:
            corner(0, blk, 0, slot).wait_recv()
            total = total + c_r[slot].astype(F32)
        return total

    def transposed(v):
        return jnp.concatenate([v, jnp.zeros((BS, 128), F32)], axis=0).T[:, 0:BS]

    nothing = jnp.zeros((BS, 128), F32)

    @pl.when(aux == 0)
    def _():
        own = transposed(gathered(mine[0], range(1, naux)))
        out_ref[0:BS, 0:BS] = own[BS:128] + gathered(nothing, range(naux, 2 * naux))[:, 0:BS]

    @pl.when(aux == end)
    def _():
        own = transposed(gathered(mine[1], range(end)))
        out_ref[2 * BS : 3 * BS, BS:128] = own[0:BS] + gathered(nothing, range(naux, 2 * naux))[:, BS:128]

    for h in halo:
        h.wait_send()
    for cp in shares:
        cp.wait_send()
    corner(0, left, end, naux).wait_send()
    corner(1, right, 0, naux).wait_send()

    @pl.when(aux != 0)
    def _():
        corner(2, blk, 0, aux).wait_send()

    @pl.when(aux != end)
    def _():
        corner(3, blk, end, aux).wait_send()

    def drain(g, carry):
        tile(0, g).wait_send()
        tile(1, g).wait_send()
        return carry

    lax.fori_loop(0, NG, drain, 0)


def solution(mesh):
    nblk, naux = mesh.shape["blk"], mesh.shape["aux"]

    def on_device(x, block_mask, density, density_mask):
        block_mask, density, density_mask = block_mask.transpose(2, 0, 1), density.T, density_mask.T
        sem = pltpu.SemaphoreType.DMA
        return pl.pallas_call(
            functools.partial(kernel, nblk, naux),
            name="exchange",
            out_shape=pltpu.VMEM((3 * BS, NB * BS // naux), F32),
            in_specs=[pl.BlockSpec(memory_space=pl.ANY)] * 4,
            out_specs=pl.BlockSpec(memory_space=pltpu.VMEM),
            scratch_shapes=[
                pltpu.VMEM(x.shape, BF),
                pltpu.VMEM(density.shape, BF),
                pltpu.SMEM(block_mask.shape, jnp.int32),
                pltpu.SMEM(density_mask.shape, jnp.int32),
                pltpu.VMEM((NB, CP, BS, 256), BF),
                pltpu.VMEM((NB, CP, BS, 256), BF),
                pltpu.VMEM((2, NC, CP, BS, 256), BF),
                pltpu.VMEM((2, NG, CP * BS, 256), BF),
                pltpu.VMEM((2, NG, CP, 32, 384), BF),
                pltpu.VMEM((2, NG, CP, 32, 384), BF),
                pltpu.VMEM((NB + 1, 256, 256), BF),
                pltpu.VMEM((NB, 32, 256), BF),
                pltpu.VMEM((2, 32, 384), BF),
                pltpu.VMEM((2, BS, 128), BF),
                pltpu.VMEM((2, BS, 128), BF),
                pltpu.VMEM((NB, BS, 128), F32),
                pltpu.VMEM((NB, BS, 128), F32),
                pltpu.VMEM((2, BS, 128), F32),
                pltpu.VMEM((NB + 1, BS, 128), F32),
                pltpu.VMEM((NB + 1, BS, 128), BF),
                pltpu.VMEM((naux - 1, 3, BS, 128), BF),
                pltpu.VMEM((2, BS, 128), F32),
                pltpu.VMEM((2, BS, 128), BF),
                pltpu.VMEM((2 * naux, BS, 128), BF),
                sem((NC,)), sem, sem((2,)), sem((2,)), sem((2,)), sem((2,)), sem((2,)), sem((2, NG)), sem((2, NG)),
                sem((naux - 1,)), sem((naux - 1,)), sem((4,)), sem((2 * naux,)),
            ],
            compiler_params=pltpu.CompilerParams(
                collective_id=0, has_side_effects=True, vmem_limit_bytes=56 * 2**20
            ),
        )(x, block_mask, density, density_mask).T

    placed = (P("aux", "blk", None), P("aux", "blk", None), P("blk", None), P("blk", None))
    return jax.shard_map(
        on_device, mesh=mesh, in_specs=placed, out_specs=P(("blk", "aux"), None), check_vma=False
    )
```

```python
import functools

import jax
import jax.numpy as jnp
from jax import lax
from jax.experimental import pallas as pl
from jax.experimental.pallas import tpu as pltpu
from jax.sharding import PartitionSpec as P

MESH = pl.DeviceIdType.MESH
NT = (((1,), (1,)), ((), ()))
BF = jnp.bfloat16
F32 = jnp.float32

NB = 8
BS = 64
CP = 4
NC = 16
NG = NC // 2


def first_place(b):
    return (b + 3) % 4


def aligned(cols, halves, place, low):
    turned = {}

    def at(half, side):
        col = half // 2
        if half % 2 == side:
            return cols[col]
        if col not in turned:
            turned[col] = pltpu.roll(cols[col], BS, 1)
        return turned[col]

    slots = [None] * 4
    for k, half in enumerate(halves):
        slots[(place + k) % 4] = half
    out = []
    for q in range(2):
        left, right = slots[2 * q], slots[2 * q + 1]
        if left is None:
            out.append(at(right, 1))
        elif right is None:
            out.append(at(left, 0))
        else:
            a, b = at(left, 0), at(right, 1)
            out.append(a if a is b else jnp.where(low, a, b))
    return out


def kernel(
    nblk, naux,
    x_hbm, bm_hbm, d_hbm, dm_hbm, out_ref,
    x_v, d_v, bm_ref, dm_ref, ta, tb, te, hx, send, recv, dens, mask, mask_s, halo_s, halo_r,
    k0, k1, kb, xf, xs, r1, mine, c_s, c_r,
    x_sem, d_sem, m_sem, hs, hr, ps, pr, bs, br, s1, rs1, s2, rs2,
):
    blk, aux = lax.axis_index("blk"), lax.axis_index("aux")
    right, left = lax.rem(blk + 1, nblk), lax.rem(blk + nblk - 1, nblk)

    def load(c):
        return pltpu.make_async_copy(x_hbm.at[pl.ds(c * CP, CP)], x_v.at[pl.ds(c * CP, CP)], x_sem.at[c])

    load(0).start()
    load(1).start()
    marks = (
        pltpu.make_async_copy(bm_hbm, bm_ref, m_sem.at[0]),
        pltpu.make_async_copy(dm_hbm, dm_ref, m_sem.at[1]),
    )
    for m in marks:
        m.start()

    barrier = pltpu.get_barrier_semaphore()
    for where in (left, blk, right):
        for k in range(naux):
            if where is blk and k == 0:
                continue
            pl.semaphore_signal(barrier, inc=1, device_id=(where, lax.rem(aux + k, naux)), device_id_type=MESH)

    density = pltpu.make_async_copy(d_hbm, d_v, d_sem)
    density.start()
    for c in range(2, NC):
        load(c).start()

    lane = lax.broadcasted_iota(jnp.int32, (32, 128), 1)
    low = lane < BS
    low64 = lax.broadcasted_iota(jnp.int32, (BS, 128), 1) < BS

    for m in marks:
        m.wait()

    def block_marks(b):
        return [bm_ref[j, 0, b].astype(F32) for j in range(3)]

    for s, b in enumerate((0, NB - 1)):
        m = block_marks(b)
        for q, (u, v) in enumerate(((0, 1), (2, 0), (1, 2))):
            mask_s[s, :, q * 128 : (q + 1) * 128] = jnp.where(low, m[u], m[v]).astype(BF)

    def to_left(src, dst, ss, rs):
        return pltpu.make_async_remote_copy(src_ref=src, dst_ref=dst, send_sem=ss, recv_sem=rs, device_id=(left, aux), device_id_type=MESH)

    def to_right(src, dst, ss, rs):
        return pltpu.make_async_remote_copy(src_ref=src, dst_ref=dst, send_sem=ss, recv_sem=rs, device_id=(right, aux), device_id_type=MESH)

    def tile(side, g):
        return pltpu.make_async_remote_copy(
            src_ref=send.at[side, g], dst_ref=recv.at[1 - side, g], send_sem=bs.at[side, g], recv_sem=br.at[1 - side, g],
            device_id=(jnp.where(side == 0, left, right), aux), device_id_type=MESH,
        )

    def extract(g, which):
        for k in range(CP):
            rows = x_v[(2 * g + which) * CP + k].reshape(NB, 32, 384)
            send[which, g, k] = rows[(0, NB - 1)[which]] * mask_s[which]

    def spread(c, t):
        for k in range(CP):
            rows = x_v[c * CP + k].reshape(NB, 32, 384)
            for b in range(NB):
                u = rows[b]
                cols = [u[:, q * 128 : (q + 1) * 128] for q in range(3)]
                for par in range(2):
                    made = aligned(cols, [3 * par + n for n in range(3)], first_place(b), low)
                    for q in range(2):
                        rows_of, lanes = slice(par * 32, (par + 1) * 32), slice(q * 128, (q + 1) * 128)
                        v = made[q] * mask[b, :, lanes]
                        t[b, k, rows_of, lanes] = v
                        if b in (0, NB - 1):
                            te[b // (NB - 1), c, k, rows_of, lanes] = v

    def pick(o, base):
        s0 = jnp.where(low64, o[base : base + 64, 0:128], o[base + 64 : base + 128, 0:128])
        s1_ = jnp.where(low64, o[base + 128 : base + 192, 128:256], o[base + 192 : base + 256, 128:256])
        return s0 + s1_

    def product(left, tile):
        return lax.dot_general(left, tile, NT, preferred_element_type=F32)

    def halved(tile, slot):
        return jnp.dot(tile, dens[slot], preferred_element_type=F32).astype(BF)

    def multiply(t):
        before = None
        for b in range(NB):
            tile = t[b].reshape(CP * BS, 256)
            if b == NB - 1:
                k1[b - 1] += pick(product(before, tile), 0)
                continue
            half = halved(tile, b)
            if b > 0:
                o = product(jnp.concatenate([half, before], axis=0), tile)
                k0[b] += pick(o, 0)
                k1[b - 1] += pick(o, CP * BS)
            before = half

    def in_rows(half):
        return jnp.dot(dens[NB + 1], half, preferred_element_type=F32).astype(BF)

    def ends(g, carry):
        for c in range(2):
            first_tile = te[0, 2 * g + c].reshape(CP * BS, 256)
            last_tile = te[1, 2 * g + c].reshape(CP * BS, 256)
            first_half, last_half = halved(first_tile, NB), halved(last_tile, NB - 1)
            k0[0] += pick(product(first_half, first_tile), 0)
            k0[NB - 1] += pick(product(last_half, last_tile), 0)
            if c == 0:
                hx[1, g] = in_rows(last_half)
            else:
                hx[0, g] = in_rows(first_half)
        return carry

    for c in range(2):
        load(c).wait()
        extract(0, c)
        if c == 0:
            pl.semaphore_wait(barrier, 3 * naux - 1)
        tile(c, 0).start()

    density.wait()
    cols = []
    for j in range(3):
        cols.append([])
        for m in range(NB // 2):
            marks_of = jnp.where(low64, dm_ref[j, 2 * m].astype(F32), dm_ref[j, 2 * m + 1].astype(F32)).astype(BF)
            cols[j].append(d_v[j * BS : (j + 1) * BS, m * 128 : (m + 1) * 128] * marks_of)
    halo_s[0] = jnp.where(low64, cols[1][0], cols[0][0])
    halo_s[1] = jnp.where(low64, cols[2][-1], cols[1][-1])
    core = lax.rem(aux, 2)
    share = pl.ds(pl.multiple_of(core * 32, 32), 32)
    halo = (
        to_left(halo_s.at[0, share], halo_r.at[0, share], hs.at[0], hr.at[0]),
        to_right(halo_s.at[1, share], halo_r.at[1, share], hs.at[1], hr.at[1]),
    )
    passed = [
        pltpu.make_async_remote_copy(
            src_ref=halo_r.at[n, share], dst_ref=halo_r.at[n, share], send_sem=ps.at[n], recv_sem=pr.at[n],
            device_id=(blk, aux + 1 - 2 * core), device_id_type=MESH,
        )
        for n in range(2)
    ]

    for h in halo:
        h.start()

    def move(g, carry):
        for c in range(2):
            load(2 * g + c).wait()
            extract(g, c)
            tile(c, g).start()
        return carry

    lax.fori_loop(1, NG, move, 0)

    def lanes_of(values, place, rows):
        spot = lax.broadcasted_iota(jnp.int32, (rows, 256), 1) // BS
        total = jnp.zeros((rows, 256), F32)
        for j, value in enumerate(values):
            total = jnp.where(spot == (place + j) % 4, value, total)
        return total.astype(BF)

    for b in range(NB):
        mask[b] = lanes_of(block_marks(b), first_place(b), 32)
    hole = [lanes_of([1.0, 1.0, 1.0], first_place(b), 32) for b in (0, NB - 1)]

    k0[...] = jnp.zeros_like(k0)
    k1[...] = jnp.zeros_like(k1)
    kb[...] = jnp.zeros_like(kb)

    def turned(v):
        full = jnp.concatenate([v.astype(F32), jnp.zeros((BS, 128), F32)], axis=0).T
        return jnp.where(low64, full[0:BS], pltpu.roll(full[BS:128], BS, 1)).astype(BF)

    none = jnp.zeros((BS, 128), BF)
    after_t, ahead_t = turned(cols[2][-1]), turned(cols[0][0])
    after_t = pltpu.roll(after_t.astype(F32), BS, 1).astype(BF)
    ahead_t = pltpu.roll(ahead_t.astype(F32), BS, 1).astype(BF)

    def entry(l, c, after, ahead):
        j = l - c + 1
        if not 0 <= j <= 2:
            return none
        if 0 <= c < NB:
            return cols[j][c // 2]
        if c == NB:
            return (after_t, after)[l - NB + 1]
        if c == NB + 1:
            return after
        if c == -1:
            return (ahead, ahead_t)[l + 1]
        return ahead

    def second_factor(slot, b, columns, after, ahead):
        for l in range(b - 1, b + 3):
            for q in range(2):
                pair = [none if l == b + 2 else entry(l, c, after, ahead) for c in sorted(columns, key=lambda c: c % 4)[2 * q : 2 * q + 2]]
                made = none if pair[0] is none and pair[1] is none else jnp.where(low64, pair[0], pair[1])
                dens[slot, (l % 4) * BS : (l % 4 + 1) * BS, q * 128 : (q + 1) * 128] = made

    for b in range(NB - 1):
        second_factor(b, b, range(b - 1, b + 3), None, none)

    spread(0, ta)

    def step(g, carry):
        spread(2 * g + 1, tb)
        multiply(ta)
        spread(jnp.minimum(2 * g + 2, NC - 1), ta)
        multiply(tb)
        return carry

    lax.fori_loop(0, NG, step, 0)

    for h, p in zip(halo, passed, strict=True):
        h.wait_recv()
        p.start()
    for p in passed:
        p.wait()
    second_factor(NB - 1, NB - 1, range(NB - 2, NB + 2), halo_r[0], None)
    second_factor(NB, 0, range(-2, 2), None, halo_r[1])
    r = lax.broadcasted_iota(jnp.int32, (256, 256), 0)
    c = lax.broadcasted_iota(jnp.int32, (256, 256), 1)
    dens[NB + 1] = jnp.where((c % BS == 32 * (r % 2) + (r % BS) // 2) & (r // BS == c // BS), 1.0, 0.0).astype(BF)
    lax.fori_loop(0, NG, ends, 0)

    def folded(a, c):
        return jnp.where(low64, a + pltpu.roll(a, BS, 1), c + pltpu.roll(c, BS, 1))

    r = lax.broadcasted_iota(jnp.int32, (BS, 128), 0)
    c = lax.broadcasted_iota(jnp.int32, (BS, 128), 1)
    row_perm = jnp.where(r == 32 * (c % 2) + c // 2, 1.0, 0.0)[:, 0:BS]
    back = row_perm.T.astype(BF)
    r = lax.broadcasted_iota(jnp.int32, (128, 128), 0)
    c = lax.broadcasted_iota(jnp.int32, (128, 128), 1)
    lane_perm = jnp.where((r % BS == 32 * (c % 2) + (c % BS) // 2) & (r // BS == c // BS), 1.0, 0.0).astype(BF)

    def natural(v):
        v = jnp.dot(v.astype(BF), lane_perm, preferred_element_type=F32).astype(BF)
        return jnp.dot(back, v, preferred_element_type=F32)

    xs[0] = jnp.zeros((BS, 128), BF)
    xf[0] = jnp.zeros((BS, 128), F32)
    for b in range(NB):
        v = natural(folded(k0[b], k1[b]))
        xf[b + 1] = v
        xs[b + 1] = v.astype(BF)
    shares = []
    for k in range(1, naux):
        to = lax.rem(aux + k, naux)
        cp = pltpu.make_async_remote_copy(
            src_ref=xs.at[pl.ds(2 * to, 3)], dst_ref=r1.at[k - 1], send_sem=s1.at[k - 1], recv_sem=rs1.at[k - 1],
            device_id=(blk, to), device_id_type=MESH,
        )
        cp.start()
        shares.append(cp)

    def edge(side, g):
        parts = []
        for k in range(CP):
            u = recv[side, g, k]
            cols = [u[:, q * 128 : (q + 1) * 128] for q in range(3)]
            for par in range(2):
                made = aligned(cols, [3 * par + n for n in range(3)], first_place((NB - 1, 0)[side]), low)
                parts.append(jnp.concatenate([made[q] * hole[1 - side][:, q * 128 : (q + 1) * 128] for q in range(2)], axis=1))
        return jnp.concatenate(parts, axis=0)

    end = naux - 1

    def corner(n, where, to, slot):
        return pltpu.make_async_remote_copy(
            src_ref=c_s.at[n % 2], dst_ref=c_r.at[slot], send_sem=s2.at[n], recv_sem=rs2.at[slot], device_id=(where, to), device_id_type=MESH
        )

    def finish(sides):
        def far(g, carry):
            for side in sides:
                tile(1 - side, g).wait_recv()
                kb[side] += pick(product(hx[side, g], edge(side, g)), 0)
            return carry

        lax.fori_loop(0, NG, far, 0)
        v = jnp.dot(folded(kb[1], kb[0]).astype(BF), lane_perm, preferred_element_type=F32)
        for side in sides:
            mine[side] = v
            c_s[side] = v.astype(BF)
        for side in sides:
            if side == 0:
                corner(0, left, end, naux + aux).start()
            else:
                corner(1, right, 0, naux + aux).start()

            @pl.when(aux != (0, end)[side])
            def _():
                corner(2 + side, blk, (0, end)[side], aux).start()

    odd = lax.rem(blk, 2) == 1

    @pl.when(odd)
    def _():
        finish((1,))
        finish((0,))

    @pl.when(jnp.logical_not(odd))
    def _():
        finish((0,))
        finish((1,))

    for cp in shares:
        cp.wait_recv()
    total = []
    for j in range(3):
        v = xf[2 * aux + j]
        for k in range(naux - 1):
            v = v + r1[k, j].astype(F32)
        total.append(v)

    out_ref[0:BS, :] = jnp.where(low64, pltpu.roll(total[0], BS, 1), total[1])
    out_ref[BS : 2 * BS, :] = jnp.where(low64, total[1], pltpu.roll(total[2], BS, 1))
    out_ref[2 * BS : 3 * BS, :] = jnp.concatenate(total[1:], axis=0).T[BS:128]

    def gathered(total, slots):
        for slot in slots:
            corner(0, blk, 0, slot).wait_recv()
            total = total + c_r[slot].astype(F32)
        return total

    def transposed(v):
        return jnp.concatenate([v, jnp.zeros((BS, 128), F32)], axis=0).T[:, 0:BS]

    nothing = jnp.zeros((BS, 128), F32)

    @pl.when(aux == 0)
    def _():
        own = transposed(gathered(mine[0], range(1, naux)))
        out_ref[0:BS, 0:BS] = own[BS:128] + gathered(nothing, range(naux, 2 * naux))[:, 0:BS]

    @pl.when(aux == end)
    def _():
        own = transposed(gathered(mine[1], range(end)))
        out_ref[2 * BS : 3 * BS, BS:128] = own[0:BS] + gathered(nothing, range(naux, 2 * naux))[:, BS:128]

    for h in halo:
        h.wait_send()
    for cp in shares:
        cp.wait_send()
    corner(0, left, end, naux).wait_send()
    corner(1, right, 0, naux).wait_send()

    @pl.when(aux != 0)
    def _():
        corner(2, blk, 0, aux).wait_send()

    @pl.when(aux != end)
    def _():
        corner(3, blk, end, aux).wait_send()

    def drain(g, carry):
        tile(0, g).wait_send()
        tile(1, g).wait_send()
        return carry

    lax.fori_loop(0, NG, drain, 0)


def solution(mesh):
    nblk, naux = mesh.shape["blk"], mesh.shape["aux"]

    def on_device(x, block_mask, density, density_mask):
        block_mask, density, density_mask = block_mask.transpose(2, 0, 1), density.T, density_mask.T
        sem = pltpu.SemaphoreType.DMA
        return pl.pallas_call(
            functools.partial(kernel, nblk, naux),
            name="exchange",
            out_shape=pltpu.VMEM((3 * BS, NB * BS // naux), F32),
            in_specs=[pl.BlockSpec(memory_space=pl.ANY)] * 4,
            out_specs=pl.BlockSpec(memory_space=pltpu.VMEM),
            scratch_shapes=[
                pltpu.VMEM(x.shape, BF),
                pltpu.VMEM(density.shape, BF),
                pltpu.SMEM(block_mask.shape, jnp.int32),
                pltpu.SMEM(density_mask.shape, jnp.int32),
                pltpu.VMEM((NB, CP, BS, 256), BF),
                pltpu.VMEM((NB, CP, BS, 256), BF),
                pltpu.VMEM((2, NC, CP, BS, 256), BF),
                pltpu.VMEM((2, NG, CP * BS, 256), BF),
                pltpu.VMEM((2, NG, CP, 32, 384), BF),
                pltpu.VMEM((2, NG, CP, 32, 384), BF),
                pltpu.VMEM((NB + 2, 256, 256), BF),
                pltpu.VMEM((NB, 32, 256), BF),
                pltpu.VMEM((2, 32, 384), BF),
                pltpu.VMEM((2, BS, 128), BF),
                pltpu.VMEM((2, BS, 128), BF),
                pltpu.VMEM((NB, BS, 128), F32),
                pltpu.VMEM((NB, BS, 128), F32),
                pltpu.VMEM((2, BS, 128), F32),
                pltpu.VMEM((NB + 1, BS, 128), F32),
                pltpu.VMEM((NB + 1, BS, 128), BF),
                pltpu.VMEM((naux - 1, 3, BS, 128), BF),
                pltpu.VMEM((2, BS, 128), F32),
                pltpu.VMEM((2, BS, 128), BF),
                pltpu.VMEM((2 * naux, BS, 128), BF),
                sem((NC,)), sem, sem((2,)), sem((2,)), sem((2,)), sem((2,)), sem((2,)), sem((2, NG)), sem((2, NG)),
                sem((naux - 1,)), sem((naux - 1,)), sem((4,)), sem((2 * naux,)),
            ],
            compiler_params=pltpu.CompilerParams(
                collective_id=0, has_side_effects=True, vmem_limit_bytes=56 * 2**20
            ),
        )(x, block_mask, density, density_mask).T

    placed = (P("aux", "blk", None), P("aux", "blk", None), P("blk", None), P("blk", None))
    return jax.shard_map(
        on_device, mesh=mesh, in_specs=placed, out_specs=P(("blk", "aux"), None), check_vma=False
    )
```
